32 devices in a mesh: tm: 8 (over z, y), chan: 4 (over x, core).
Axes of the slice: x: 2, y: 2, z: 4, core: 2. Of those that a mesh axis runs over, the one named last changes fastest.
Arguments:
- record: bfloat16 [1280, 8192], P('chan', 'tm'), may hold values from -200 to 200
- owner: int32 [4], replicated, may hold values from 0 to 7, as said below
- offsets: int32 [4, 16], replicated, may hold values from 0 to 924
Outputs:
- score: float32 [4, 16, 8192], P(None, None, 'tm')
The draws below stay inside these ranges and needn't reach their ends.
Inputs may be any that keep to these rules, and one draw needn't show every extreme that they name: `owner`: no two batches share a time block, and one batch is always held by the last block. `offsets`: a template lies wholly inside its owner's block.
All inputs are finite; a program needn't handle non-finite values.
Results may differ from the reference program's by a relative error of at most 0.0003.
Values may be sent and summed in bfloat16 or wider, within the bound.
A program may use at most 64 MiB of HBM per device.

```python
import jax
import jax.numpy as jnp
from jax import lax

TDEV = 1024
L = 100
K = 16
NB = 4
CHANNELS = 1280
SAMPLES = 8192
N_TM = 8


def draw_record(key, part):
    keys = jax.random.split(key, 4)
    position = jnp.arange(CHANNELS, dtype=jnp.float32) / CHANNELS
    spread = 0.7
    noise = jax.random.normal(keys[0], (CHANNELS, SAMPLES), jnp.float32)
    gain = jnp.exp(0.55 * position + jax.random.uniform(keys[1], (CHANNELS,), jnp.float32, -spread, spread))
    wave = jax.random.normal(keys[2], (SAMPLES,), jnp.float32)
    pace = jnp.exp(jax.random.uniform(keys[3], (SAMPLES,), jnp.float32, -0.5, 0.5))
    values = gain[:, None] * pace[None, :] * (0.8 * wave[None, :] + noise)
    return jnp.clip(values, -200.0, 200.0).astype(jnp.bfloat16)


def draw_owner(key, part):
    others = jax.random.permutation(jax.random.fold_in(key, 11), N_TM - 1)[:NB - 1].astype(jnp.int32)
    chosen = jnp.concatenate([others, jnp.full((1,), N_TM - 1, jnp.int32)])
    order = jax.random.permutation(jax.random.fold_in(key, 12), NB)
    return chosen[order].astype(jnp.int32)


def set_ends(entries, rng, least, high):
    place = [jax.random.randint(jax.random.fold_in(rng, axis), (), 0, length) for axis, length in enumerate(entries.shape)]
    longest = entries.shape.index(max(entries.shape))
    next_to = place[:longest] + [(place[longest] + 1) % entries.shape[longest]] + place[longest + 1:]
    return entries.at[tuple(place)].set(least).at[tuple(next_to)].set(high)


def setup_inputs(seed: int = 0) -> dict:
    splits = jax.random.split(jax.random.key(seed), 4)
    record = draw_record(jax.random.fold_in(splits[3], 71), 0)
    owner = draw_owner(jax.random.fold_in(splits[3], 71), 0)
    offsets = set_ends(jax.random.randint(splits[2], (NB, K), 0, TDEV - L + 1), jax.random.fold_in(splits[2], 1), 0, TDEV - L).astype(jnp.int32)
    return dict(record=record, owner=owner, offsets=offsets)


def reference(record, owner, offsets):
    full = record.astype(jnp.float32)
    starts = (owner[:, None] * TDEV + offsets).reshape(-1).astype(jnp.int32)
    windows = jax.vmap(lambda s: lax.dynamic_slice_in_dim(full, s, L, 1))(starts)
    padded = jnp.pad(full, ((0, 0), (0, L - 1)))

    def tap_step(j, acc):
        weights = lax.dynamic_index_in_dim(windows, j, 2, keepdims=False)
        shifted = lax.dynamic_slice_in_dim(padded, j, SAMPLES, 1)
        return acc + jnp.dot(weights, shifted, preferred_element_type=jnp.float32, precision=lax.Precision.HIGHEST)
    corr = lax.fori_loop(0, L, tap_step, jnp.zeros((NB * K, SAMPLES), jnp.float32))
    squares = lax.optimization_barrier(jnp.sum(padded * padded, axis=0))
    running = jnp.concatenate([jnp.zeros((1,), jnp.float32), jnp.cumsum(squares)])
    energy = running[L:L + SAMPLES] - running[:SAMPLES]
    tnorm = lax.optimization_barrier(jnp.sum(windows * windows, axis=(1, 2)))
    score = corr / jnp.sqrt((energy[None, :] + 1e-05) * tnorm[:, None])
    return score.reshape(NB, K, SAMPLES)
```

```python
import functools

import jax
import jax.numpy as jnp
from jax import lax
from jax.experimental import pallas as pl
from jax.experimental.pallas import tpu as pltpu
from jax.sharding import PartitionSpec as P

L = 100
FOLD = 8
STEPS = -(-L // FOLD)
RIM = 128
LANES = 256
SUB = 5
MESH = pl.DeviceIdType.MESH
VMEM = pl.BlockSpec(memory_space=pltpu.VMEM)
SMEM = pl.BlockSpec(memory_space=pltpu.SMEM)


def gather_kernel(pairs, batches, owner_ref, x_ref, ext_ref, blocks_ref,
                  own, rim, from_l, from_r, to_r, to_l,
                  pair_sem, rim_sem, rs, rr, ls, lr):
    tm = lax.axis_index("tm")
    p, h = tm // 2, tm % 2
    peer = tm + 1 - 2 * h
    half = own.shape[1]
    width = own.shape[2]
    rows = half // SUB
    chunks = batches * SUB
    has_l, has_r = p > 0, p < pairs - 1

    barrier = pltpu.get_barrier_semaphore()
    pl.semaphore_signal(barrier, inc=1, device_id={"tm": peer}, device_id_type=MESH)

    @pl.when(has_l)
    def _():
        pl.semaphore_signal(barrier, inc=1, device_id={"tm": tm - 2}, device_id_type=MESH)

    @pl.when(has_r)
    def _():
        pl.semaphore_signal(barrier, inc=1, device_id={"tm": tm + 2}, device_id_type=MESH)

    pl.semaphore_wait(barrier, 1 + has_l.astype(jnp.int32) + has_r.astype(jnp.int32))

    swap = pltpu.make_async_remote_copy(
        src_ref=x_ref.at[pl.ds(pl.multiple_of((1 - h) * half, 16), half)],
        dst_ref=own.at[h],
        send_sem=pair_sem.at[0], recv_sem=pair_sem.at[1],
        device_id={"tm": peer}, device_id_type=MESH)
    swap.start()
    keep = pltpu.make_async_copy(
        x_ref.at[pl.ds(pl.multiple_of(h * half, 16), half)], own.at[h], pair_sem.at[2])
    keep.start()
    keep.wait()

    @pl.when(jnp.logical_not(has_l))
    def _():
        from_l[...] = jnp.zeros_like(from_l)

    @pl.when(jnp.logical_not(has_r))
    def _():
        from_r[...] = jnp.zeros_like(from_r)
        rim[...] = jnp.zeros_like(rim)

    swap.wait()

    rim_copy = pltpu.make_async_remote_copy(
        src_ref=own.at[0, :, pl.ds(0, RIM)], dst_ref=rim,
        send_sem=rim_sem.at[0], recv_sem=rim_sem.at[1],
        device_id={"tm": tm - 2}, device_id_type=MESH)

    @pl.when(has_l)
    def _():
        rim_copy.start()

    def right(i):
        return pltpu.make_async_remote_copy(
            src_ref=to_r.at[i], dst_ref=from_l.at[i], send_sem=rs.at[i], recv_sem=rr.at[i],
            device_id={"tm": tm + 2}, device_id_type=MESH)

    def left(i):
        return pltpu.make_async_remote_copy(
            src_ref=to_l.at[i], dst_ref=from_r.at[i], send_sem=ls.at[i], recv_sem=lr.at[i],
            device_id={"tm": tm - 2}, device_id_type=MESH)

    def mine(i):
        who = owner_ref[i // SUB]
        at = pl.ds(pl.multiple_of((i % SUB) * rows, 16), rows)
        return who, jnp.where(who % 2 == 0, own[0, at, :], own[1, at, :])

    def tick(t, carry):
        i = t - p

        @pl.when(jnp.logical_and(i >= 0, i < chunks))
        def _():
            @pl.when(has_l)
            def _():
                right(i).wait_recv()

            @pl.when(has_r)
            def _():
                who, value = mine(i)
                to_r[i] = jnp.where(who // 2 == p, value, from_l[i])
                right(i).start()

        k = t - (pairs - 1 - p)

        @pl.when(jnp.logical_and(k >= 0, k < chunks))
        def _():
            @pl.when(has_r)
            def _():
                left(k).wait_recv()

            @pl.when(has_l)
            def _():
                who, value = mine(k)
                to_l[k] = jnp.where(who // 2 == p, value, from_r[k])
                left(k).start()

        return carry

    lax.fori_loop(0, chunks + pairs - 1, tick, 0)

    def settle(i, carry):
        who, value = mine(i)
        far = jnp.where(who // 2 < p, from_l[i], from_r[i])
        at = pl.ds(pl.multiple_of((i % SUB) * rows, 16), rows)
        blocks_ref[i // SUB, at, :] = jnp.where(who // 2 == p, value, far)
        return carry

    lax.fori_loop(0, chunks, settle, 0)

    @pl.when(has_r)
    def _():
        rim_copy.wait_recv()

    ext_ref[:, :width] = own[0]
    ext_ref[:, width:2 * width] = own[1]
    ext_ref[:, 2 * width:] = rim[...]

    def drain(i, carry):
        @pl.when(has_r)
        def _():
            right(i).wait_send()

        @pl.when(has_l)
        def _():
            left(i).wait_send()

        return carry

    lax.fori_loop(0, chunks, drain, 0)

    @pl.when(has_l)
    def _():
        rim_copy.wait_send()


def gather(owner, record, pairs, batches):
    width, samples = record.shape
    half = width // 2
    chunks = batches * SUB
    slots = pltpu.VMEM((chunks, half // SUB, samples), record.dtype)
    sems = pltpu.SemaphoreType.DMA((chunks,))
    return pl.pallas_call(
        functools.partial(gather_kernel, pairs, batches),
        out_shape=(jax.ShapeDtypeStruct((half, 2 * samples + RIM), record.dtype),
                   jax.ShapeDtypeStruct((batches, half, samples), record.dtype)),
        in_specs=[SMEM, VMEM],
        out_specs=(VMEM, VMEM),
        scratch_shapes=[pltpu.VMEM((2, half, samples), record.dtype),
                        pltpu.VMEM((half, RIM), record.dtype),
                        slots, slots, slots, slots,
                        pltpu.SemaphoreType.DMA((3,)), pltpu.SemaphoreType.DMA((2,)),
                        sems, sems, sems, sems],
        compiler_params=pltpu.CompilerParams(
            collective_id=0, has_side_effects=True, vmem_limit_bytes=40 << 20),
        name="gather_blocks",
    )(owner, record)


def correlate_kernel(per_batch, index_ref, ext_ref, block_ref, corr_ref, energy_ref, tnorm_ref,
                     stack, weights):
    half, span = ext_ref.shape
    samples = block_ref.shape[2]
    reach = corr_ref.shape[2]

    @pl.when(pl.program_id(0) == 0)
    def _():
        wide = ext_ref[...].astype(jnp.float32)
        stack[:half] = ext_ref[...]
        for j in range(1, FOLD):
            stack[j * half:(j + 1) * half] = pltpu.roll(wide, span - j, 1).astype(jnp.bfloat16)
        sums = {1: jnp.broadcast_to(jnp.sum(wide * wide, axis=0, keepdims=True), (8, span))}
        n = 1
        while 2 * n <= L:
            sums[2 * n] = sums[n] + pltpu.roll(sums[n], span - n, 1)
            n *= 2
        done, total = 0, None
        for n in sorted(sums, reverse=True):
            if n & L:
                term = sums[n] if done == 0 else pltpu.roll(sums[n], span - done, 1)
                total = term if total is None else total + term
                done += n
        energy_ref[...] = total[:, :reach]

    block = block_ref[0]
    row = lax.broadcasted_iota(jnp.int32, (samples, LANES), 0)
    norm = jnp.zeros((1, LANES), jnp.float32)
    for j in range(FOLD):
        hot = jnp.where(row == index_ref[0, j:j + 1, :], 1.0, 0.0).astype(jnp.bfloat16)
        part = jnp.dot(block, hot, preferred_element_type=jnp.float32)
        norm = norm + jnp.sum(part * part, axis=0, keepdims=True)
        weights[j * half:(j + 1) * half] = part.astype(jnp.bfloat16)
    tnorm_ref[0] = norm
    used = STEPS * per_batch
    turned = weights[...].T[:used]
    grid = jnp.dot(turned, stack[...], preferred_element_type=jnp.float32)
    acc = grid[:per_batch]
    for s in range(1, STEPS):
        acc = acc + pltpu.roll(grid[s * per_batch:(s + 1) * per_batch], span - s * FOLD, 1)
    corr_ref[0] = acc[:, :reach]


def correlate(index, ext, blocks, per_batch):
    batches, half, samples = blocks.shape
    span = ext.shape[1]
    reach = span - RIM
    return pl.pallas_call(
        functools.partial(correlate_kernel, per_batch),
        grid=(batches,),
        out_shape=(jax.ShapeDtypeStruct((batches, per_batch, reach), jnp.float32),
                   jax.ShapeDtypeStruct((8, reach), jnp.float32),
                   jax.ShapeDtypeStruct((batches, 1, LANES), jnp.float32)),
        in_specs=[pl.BlockSpec((1, FOLD, LANES), lambda b: (b, 0, 0)),
                  pl.BlockSpec((half, span), lambda b: (0, 0)),
                  pl.BlockSpec((1, half, samples), lambda b: (b, 0, 0))],
        out_specs=(pl.BlockSpec((1, per_batch, reach), lambda b: (b, 0, 0)),
                   pl.BlockSpec((8, reach), lambda b: (0, 0)),
                   pl.BlockSpec((1, 1, LANES), lambda b: (b, 0, 0))),
        scratch_shapes=[pltpu.VMEM((FOLD * half, span), jnp.bfloat16),
                        pltpu.VMEM((FOLD * half, LANES), jnp.bfloat16)],
        compiler_params=pltpu.CompilerParams(
            dimension_semantics=("arbitrary",), vmem_limit_bytes=48 << 20),
        name="correlate_batches",
    )(index, ext, blocks)


def sum_kernel(peers, part_ref, aux_ref, corr_ref, out_aux_ref,
               got, got_aux, s1, r1, s2, r2, s3, r3):
    tm, c = lax.axis_index("tm"), lax.axis_index("chan")
    h = tm % 2
    samples = corr_ref.shape[2]
    me = h * peers + c
    team = 2 * peers

    def member(i):
        m = lax.rem(me + i, team)
        return m // peers, m % peers

    def target(i):
        hh, cc = member(i)
        return {"tm": tm - h + hh, "chan": cc}

    barrier = pltpu.get_barrier_semaphore()
    for i in range(1, team):
        pl.semaphore_signal(barrier, inc=1, device_id=target(i), device_id_type=MESH)
    pl.semaphore_wait(barrier, team - 1)

    def piece(i):
        hh, cc = member(i)
        return pltpu.make_async_remote_copy(
            src_ref=part_ref.at[cc, :, pl.ds(pl.multiple_of(hh * samples, 128), samples)],
            dst_ref=got.at[i], send_sem=s1.at[i], recv_sem=r1.at[i],
            device_id=target(i), device_id_type=MESH)

    def extra(i):
        hh, cc = member(i)
        return pltpu.make_async_remote_copy(
            src_ref=aux_ref.at[hh], dst_ref=got_aux.at[me], send_sem=s2.at[i], recv_sem=r2.at[i],
            device_id=target(i), device_id_type=MESH)

    def extra_from(i):
        whose = lax.rem(me + team - i, team)
        return pltpu.make_async_remote_copy(
            src_ref=aux_ref.at[0], dst_ref=got_aux.at[whose], send_sem=s2.at[i],
            recv_sem=r2.at[i], device_id=target(i), device_id_type=MESH)

    def share(i):
        return pltpu.make_async_remote_copy(
            src_ref=corr_ref.at[c], dst_ref=corr_ref.at[c], send_sem=s3.at[i], recv_sem=r3.at[i],
            device_id={"tm": tm, "chan": lax.rem(c + i, peers)}, device_id_type=MESH)

    def arriving(i):
        whose = lax.rem(c + peers - i, peers)
        return pltpu.make_async_remote_copy(
            src_ref=corr_ref.at[whose], dst_ref=corr_ref.at[whose], send_sem=s3.at[i],
            recv_sem=r3.at[i], device_id={"tm": tm, "chan": whose}, device_id_type=MESH)

    for i in range(1, team):
        piece(i).start()
    for i in range(1, team):
        extra(i).start()
    total = part_ref[c, :, pl.ds(pl.multiple_of(h * samples, 128), samples)]
    for i in range(1, team):
        piece(i).wait_recv()
        total = total + got[i]
    corr_ref[c] = total
    for i in range(1, peers):
        share(i).start()
    got_aux[me] = aux_ref[h]
    for i in range(1, team):
        extra_from(i).wait_recv()
    aux = got_aux[0]
    for i in range(1, team):
        aux = aux + got_aux[i]
    out_aux_ref[...] = aux
    for i in range(1, peers):
        arriving(i).wait_recv()
    for i in range(1, peers):
        share(i).wait_send()
    for i in range(1, team):
        piece(i).wait_send()
        extra(i).wait_send()


def reduce_all(part, aux, peers):
    _, rows, reach = part.shape
    samples = reach // 2
    team = 2 * peers
    many = pltpu.SemaphoreType.DMA((team,))
    few = pltpu.SemaphoreType.DMA((peers,))
    return pl.pallas_call(
        functools.partial(sum_kernel, peers),
        out_shape=(jax.ShapeDtypeStruct((peers, rows, samples), jnp.float32),
                   jax.ShapeDtypeStruct(aux.shape[1:], jnp.float32)),
        in_specs=[VMEM, VMEM],
        out_specs=(VMEM, VMEM),
        scratch_shapes=[pltpu.VMEM((team, rows, samples), jnp.float32),
                        pltpu.VMEM((team,) + aux.shape[1:], jnp.float32),
                        many, many, many, many, few, few],
        compiler_params=pltpu.CompilerParams(
            collective_id=1, has_side_effects=True, vmem_limit_bytes=32 << 20),
        name="sum_channels",
    )(part, aux)


def on_device(pairs, peers, record, owner, offsets):
    samples = record.shape[1]
    batches, per_batch = offsets.shape
    lane = jnp.arange(LANES)
    tap = FOLD * (lane // per_batch)[None, :] + jnp.arange(FOLD)[:, None]
    start = offsets[:, lane % per_batch]
    index = jnp.where(tap[None] < L, start[:, None, :] + tap[None], -1).astype(jnp.int32)

    ext, blocks = gather(owner, record, pairs, batches)
    corr, energy, norms = correlate(index, ext, blocks, per_batch)
    energy = energy[0].reshape(2, samples // 128, 128)
    norms = jnp.broadcast_to(norms.reshape(1, batches * LANES // 128, 128),
                             (2, batches * LANES // 128, 128))
    aux = jnp.concatenate([energy, norms], axis=1)
    part = corr.reshape(peers, batches * per_batch // peers, 2 * samples)
    total, aux = reduce_all(part, aux, peers)
    energy = aux[:samples // 128].reshape(samples)
    norms = aux[samples // 128:].reshape(batches, LANES // per_batch, per_batch).sum(axis=1)
    total = total.reshape(batches, per_batch, samples)
    return total / jnp.sqrt((energy + 1e-05)[None, None, :] * norms[:, :, None])


def solution(mesh):
    run = functools.partial(on_device, mesh.shape["tm"] // 2, mesh.shape["chan"])
    return jax.shard_map(
        run, mesh=mesh, in_specs=(P("chan", "tm"), P(), P()),
        out_specs=P(None, None, "tm"), check_vma=False)
```

```python
import functools

import jax
import jax.numpy as jnp
from jax import lax
from jax.experimental import pallas as pl
from jax.experimental.pallas import tpu as pltpu
from jax.sharding import PartitionSpec as P

L = 100
FOLD = 8
STEPS = -(-L // FOLD)
RIM = 128
LANES = 256
SUB = 5
SLACK = 3
MESH = pl.DeviceIdType.MESH
VMEM = pl.BlockSpec(memory_space=pltpu.VMEM)
SMEM = pl.BlockSpec(memory_space=pltpu.SMEM)


def gather_kernel(pairs, batches, owner_ref, x_ref, ext_ref, blocks_ref,
                  own, rim, from_l, from_r, to_r, to_l,
                  keep_sem, rim_sem, swap_s, swap_r, rs, rr, ls, lr):
    tm = lax.axis_index("tm")
    p, h = tm // 2, tm % 2
    peer = tm + 1 - 2 * h
    half = own.shape[1]
    width = own.shape[2]
    rows = half // SUB
    chunks = batches * SUB
    has_l, has_r = p > 0, p < pairs - 1

    barrier = pltpu.get_barrier_semaphore()
    pl.semaphore_signal(barrier, inc=1, device_id={"tm": peer}, device_id_type=MESH)

    @pl.when(has_l)
    def _():
        pl.semaphore_signal(barrier, inc=1, device_id={"tm": tm - 2}, device_id_type=MESH)

    @pl.when(has_r)
    def _():
        pl.semaphore_signal(barrier, inc=1, device_id={"tm": tm + 2}, device_id_type=MESH)

    pl.semaphore_wait(barrier, 1 + has_l.astype(jnp.int32) + has_r.astype(jnp.int32))

    def swap(q):
        return pltpu.make_async_remote_copy(
            src_ref=x_ref.at[pl.ds(pl.multiple_of((1 - h) * half + q * rows, 16), rows)],
            dst_ref=own.at[h, pl.ds(pl.multiple_of(q * rows, 16), rows)],
            send_sem=swap_s.at[q], recv_sem=swap_r.at[q],
            device_id={"tm": peer}, device_id_type=MESH)

    def swapped(q):
        return pltpu.make_async_remote_copy(
            src_ref=x_ref.at[pl.ds(pl.multiple_of((1 - h) * half + q * rows, 16), rows)],
            dst_ref=own.at[1 - h, pl.ds(pl.multiple_of(q * rows, 16), rows)],
            send_sem=swap_s.at[q], recv_sem=swap_r.at[q],
            device_id={"tm": peer}, device_id_type=MESH)

    def send_swap(q, carry):
        swap(q).start()
        return carry

    lax.fori_loop(0, SUB, send_swap, 0)
    keep = pltpu.make_async_copy(
        x_ref.at[pl.ds(pl.multiple_of(h * half, 16), half)], own.at[h], keep_sem)
    keep.start()
    keep.wait()

    @pl.when(jnp.logical_not(has_l))
    def _():
        from_l[...] = jnp.zeros_like(from_l)

    @pl.when(jnp.logical_not(has_r))
    def _():
        from_r[...] = jnp.zeros_like(from_r)
        rim[...] = jnp.zeros_like(rim)

    rim_copy = pltpu.make_async_remote_copy(
        src_ref=own.at[0, :, pl.ds(0, RIM)], dst_ref=rim,
        send_sem=rim_sem.at[0], recv_sem=rim_sem.at[1],
        device_id={"tm": tm - 2}, device_id_type=MESH)

    def right(i):
        return pltpu.make_async_remote_copy(
            src_ref=to_r.at[i], dst_ref=from_l.at[i], send_sem=rs.at[i], recv_sem=rr.at[i],
            device_id={"tm": tm + 2}, device_id_type=MESH)

    def left(i):
        return pltpu.make_async_remote_copy(
            src_ref=to_l.at[i], dst_ref=from_r.at[i], send_sem=ls.at[i], recv_sem=lr.at[i],
            device_id={"tm": tm - 2}, device_id_type=MESH)

    def mine(i):
        who = owner_ref[i // SUB]
        at = pl.ds(pl.multiple_of((i % SUB) * rows, 16), rows)
        return who, jnp.where(who % 2 == 0, own[0, at, :], own[1, at, :])

    def tick(t, carry):
        @pl.when(t < SUB)
        def _():
            swapped(t).wait_recv()

        @pl.when(jnp.logical_and(t == SUB, has_l))
        def _():
            rim_copy.start()

        i = t - p * SLACK

        @pl.when(jnp.logical_and(i >= 0, i < chunks))
        def _():
            @pl.when(has_l)
            def _():
                right(i).wait_recv()

            @pl.when(has_r)
            def _():
                who, value = mine(i)
                to_r[i] = jnp.where(who // 2 == p, value, from_l[i])
                right(i).start()

        k = t - (pairs - 1 - p) * SLACK

        @pl.when(jnp.logical_and(k >= 0, k < chunks))
        def _():
            @pl.when(has_r)
            def _():
                left(k).wait_recv()

            @pl.when(has_l)
            def _():
                who, value = mine(k)
                to_l[k] = jnp.where(who // 2 == p, value, from_r[k])
                left(k).start()

        return carry

    lax.fori_loop(0, chunks + (pairs - 1) * SLACK, tick, 0)

    def settle(i, carry):
        who, value = mine(i)
        far = jnp.where(who // 2 < p, from_l[i], from_r[i])
        at = pl.ds(pl.multiple_of((i % SUB) * rows, 16), rows)
        blocks_ref[i // SUB, at, :] = jnp.where(who // 2 == p, value, far)
        return carry

    lax.fori_loop(0, chunks, settle, 0)

    @pl.when(has_r)
    def _():
        rim_copy.wait_recv()

    ext_ref[:, :width] = own[0]
    ext_ref[:, width:2 * width] = own[1]
    ext_ref[:, 2 * width:] = rim[...]

    def drain(i, carry):
        @pl.when(has_r)
        def _():
            right(i).wait_send()

        @pl.when(has_l)
        def _():
            left(i).wait_send()

        return carry

    lax.fori_loop(0, chunks, drain, 0)

    def drain_swap(q, carry):
        swap(q).wait_send()
        return carry

    lax.fori_loop(0, SUB, drain_swap, 0)

    @pl.when(has_l)
    def _():
        rim_copy.wait_send()


def gather(owner, record, pairs, batches):
    width, samples = record.shape
    half = width // 2
    chunks = batches * SUB
    slots = pltpu.VMEM((chunks, half // SUB, samples), record.dtype)
    sems = pltpu.SemaphoreType.DMA((chunks,))
    return pl.pallas_call(
        functools.partial(gather_kernel, pairs, batches),
        out_shape=(jax.ShapeDtypeStruct((half, 2 * samples + RIM), record.dtype),
                   jax.ShapeDtypeStruct((batches, half, samples), record.dtype)),
        in_specs=[SMEM, VMEM],
        out_specs=(VMEM, VMEM),
        scratch_shapes=[pltpu.VMEM((2, half, samples), record.dtype),
                        pltpu.VMEM((half, RIM), record.dtype),
                        slots, slots, slots, slots,
                        pltpu.SemaphoreType.DMA, pltpu.SemaphoreType.DMA((2,)),
                        pltpu.SemaphoreType.DMA((SUB,)), pltpu.SemaphoreType.DMA((SUB,)),
                        sems, sems, sems, sems],
        compiler_params=pltpu.CompilerParams(
            collective_id=0, has_side_effects=True, vmem_limit_bytes=40 << 20),
        name="gather_blocks",
    )(owner, record)


def correlate_kernel(per_batch, index_ref, ext_ref, block_ref, corr_ref, energy_ref, tnorm_ref,
                     stack, weights):
    half, span = ext_ref.shape
    samples = block_ref.shape[2]
    reach = corr_ref.shape[2]

    @pl.when(pl.program_id(0) == 0)
    def _():
        wide = ext_ref[...].astype(jnp.float32)
        stack[:half] = ext_ref[...]
        for j in range(1, FOLD):
            stack[j * half:(j + 1) * half] = pltpu.roll(wide, span - j, 1).astype(jnp.bfloat16)
        sums = {1: jnp.broadcast_to(jnp.sum(wide * wide, axis=0, keepdims=True), (8, span))}
        n = 1
        while 2 * n <= L:
            sums[2 * n] = sums[n] + pltpu.roll(sums[n], span - n, 1)
            n *= 2
        done, total = 0, None
        for n in sorted(sums, reverse=True):
            if n & L:
                term = sums[n] if done == 0 else pltpu.roll(sums[n], span - done, 1)
                total = term if total is None else total + term
                done += n
        energy_ref[...] = total[:, :reach]

    block = block_ref[0]
    row = lax.broadcasted_iota(jnp.int32, (samples, LANES), 0)
    norm = jnp.zeros((1, LANES), jnp.float32)
    for j in range(FOLD):
        hot = jnp.where(row == index_ref[0, j:j + 1, :], 1.0, 0.0).astype(jnp.bfloat16)
        part = jnp.dot(block, hot, preferred_element_type=jnp.float32)
        norm = norm + jnp.sum(part * part, axis=0, keepdims=True)
        weights[j * half:(j + 1) * half] = part.astype(jnp.bfloat16)
    tnorm_ref[0] = norm
    used = STEPS * per_batch
    turned = weights[...].T[:used]
    grid = jnp.dot(turned, stack[...], preferred_element_type=jnp.float32)
    acc = grid[:per_batch]
    for s in range(1, STEPS):
        acc = acc + pltpu.roll(grid[s * per_batch:(s + 1) * per_batch], span - s * FOLD, 1)
    corr_ref[0] = acc[:, :reach]


def correlate(index, ext, blocks, per_batch):
    batches, half, samples = blocks.shape
    span = ext.shape[1]
    reach = span - RIM
    return pl.pallas_call(
        functools.partial(correlate_kernel, per_batch),
        grid=(batches,),
        out_shape=(jax.ShapeDtypeStruct((batches, per_batch, reach), jnp.float32),
                   jax.ShapeDtypeStruct((8, reach), jnp.float32),
                   jax.ShapeDtypeStruct((batches, 1, LANES), jnp.float32)),
        in_specs=[pl.BlockSpec((1, FOLD, LANES), lambda b: (b, 0, 0)),
                  pl.BlockSpec((half, span), lambda b: (0, 0)),
                  pl.BlockSpec((1, half, samples), lambda b: (b, 0, 0))],
        out_specs=(pl.BlockSpec((1, per_batch, reach), lambda b: (b, 0, 0)),
                   pl.BlockSpec((8, reach), lambda b: (0, 0)),
                   pl.BlockSpec((1, 1, LANES), lambda b: (b, 0, 0))),
        scratch_shapes=[pltpu.VMEM((FOLD * half, span), jnp.bfloat16),
                        pltpu.VMEM((FOLD * half, LANES), jnp.bfloat16)],
        compiler_params=pltpu.CompilerParams(
            dimension_semantics=("arbitrary",), vmem_limit_bytes=48 << 20),
        name="correlate_batches",
    )(index, ext, blocks)


def sum_kernel(peers, part_ref, aux_ref, corr_ref, out_aux_ref,
               got, got_aux, s1, r1, s2, r2, s3, r3):
    tm, c = lax.axis_index("tm"), lax.axis_index("chan")
    h = tm % 2
    samples = corr_ref.shape[2]
    me = h * peers + c
    team = 2 * peers

    def member(i):
        m = lax.rem(me + i, team)
        return m // peers, m % peers

    def target(i):
        hh, cc = member(i)
        return {"tm": tm - h + hh, "chan": cc}

    barrier = pltpu.get_barrier_semaphore()
    for i in range(1, team):
        pl.semaphore_signal(barrier, inc=1, device_id=target(i), device_id_type=MESH)
    pl.semaphore_wait(barrier, team - 1)

    def piece(i):
        hh, cc = member(i)
        return pltpu.make_async_remote_copy(
            src_ref=part_ref.at[cc, :, pl.ds(pl.multiple_of(hh * samples, 128), samples)],
            dst_ref=got.at[i], send_sem=s1.at[i], recv_sem=r1.at[i],
            device_id=target(i), device_id_type=MESH)

    def extra(i):
        hh, cc = member(i)
        return pltpu.make_async_remote_copy(
            src_ref=aux_ref.at[hh], dst_ref=got_aux.at[me], send_sem=s2.at[i], recv_sem=r2.at[i],
            device_id=target(i), device_id_type=MESH)

    def extra_from(i):
        whose = lax.rem(me + team - i, team)
        return pltpu.make_async_remote_copy(
            src_ref=aux_ref.at[0], dst_ref=got_aux.at[whose], send_sem=s2.at[i],
            recv_sem=r2.at[i], device_id=target(i), device_id_type=MESH)

    def share(i):
        return pltpu.make_async_remote_copy(
            src_ref=corr_ref.at[c], dst_ref=corr_ref.at[c], send_sem=s3.at[i], recv_sem=r3.at[i],
            device_id={"tm": tm, "chan": lax.rem(c + i, peers)}, device_id_type=MESH)

    def arriving(i):
        whose = lax.rem(c + peers - i, peers)
        return pltpu.make_async_remote_copy(
            src_ref=corr_ref.at[whose], dst_ref=corr_ref.at[whose], send_sem=s3.at[i],
            recv_sem=r3.at[i], device_id={"tm": tm, "chan": whose}, device_id_type=MESH)

    for i in range(1, team):
        piece(i).start()
    for i in range(1, team):
        extra(i).start()
    total = part_ref[c, :, pl.ds(pl.multiple_of(h * samples, 128), samples)]
    for i in range(1, team):
        piece(i).wait_recv()
        total = total + got[i]
    corr_ref[c] = total
    for i in range(1, peers):
        share(i).start()
    got_aux[me] = aux_ref[h]
    for i in range(1, team):
        extra_from(i).wait_recv()
    aux = got_aux[0]
    for i in range(1, team):
        aux = aux + got_aux[i]
    out_aux_ref[...] = aux
    for i in range(1, peers):
        arriving(i).wait_recv()
    for i in range(1, peers):
        share(i).wait_send()
    for i in range(1, team):
        piece(i).wait_send()
        extra(i).wait_send()


def reduce_all(part, aux, peers):
    _, rows, reach = part.shape
    samples = reach // 2
    team = 2 * peers
    many = pltpu.SemaphoreType.DMA((team,))
    few = pltpu.SemaphoreType.DMA((peers,))
    return pl.pallas_call(
        functools.partial(sum_kernel, peers),
        out_shape=(jax.ShapeDtypeStruct((peers, rows, samples), jnp.float32),
                   jax.ShapeDtypeStruct(aux.shape[1:], jnp.float32)),
        in_specs=[VMEM, VMEM],
        out_specs=(VMEM, VMEM),
        scratch_shapes=[pltpu.VMEM((team, rows, samples), jnp.float32),
                        pltpu.VMEM((team,) + aux.shape[1:], jnp.float32),
                        many, many, many, many, few, few],
        compiler_params=pltpu.CompilerParams(
            collective_id=1, has_side_effects=True, vmem_limit_bytes=32 << 20),
        name="sum_channels",
    )(part, aux)


def on_device(pairs, peers, record, owner, offsets):
    samples = record.shape[1]
    batches, per_batch = offsets.shape
    lane = jnp.arange(LANES)
    tap = FOLD * (lane // per_batch)[None, :] + jnp.arange(FOLD)[:, None]
    start = offsets[:, lane % per_batch]
    index = jnp.where(tap[None] < L, start[:, None, :] + tap[None], -1).astype(jnp.int32)

    ext, blocks = gather(owner, record, pairs, batches)
    corr, energy, norms = correlate(index, ext, blocks, per_batch)
    energy = energy[0].reshape(2, samples // 128, 128)
    norms = jnp.broadcast_to(norms.reshape(1, batches * LANES // 128, 128),
                             (2, batches * LANES // 128, 128))
    aux = jnp.concatenate([energy, norms], axis=1)
    part = corr.reshape(peers, batches * per_batch // peers, 2 * samples)
    total, aux = reduce_all(part, aux, peers)
    energy = aux[:samples // 128].reshape(samples)
    norms = aux[samples // 128:].reshape(batches, LANES // per_batch, per_batch).sum(axis=1)
    total = total.reshape(batches, per_batch, samples)
    return total / jnp.sqrt((energy + 1e-05)[None, None, :] * norms[:, :, None])


def solution(mesh):
    run = functools.partial(on_device, mesh.shape["tm"] // 2, mesh.shape["chan"])
    return jax.shard_map(
        run, mesh=mesh, in_specs=(P("chan", "tm"), P(), P()),
        out_specs=P(None, None, "tm"), check_vma=False)
```

```python
import functools

import jax
import jax.numpy as jnp
from jax import lax
from jax.experimental import pallas as pl
from jax.experimental.pallas import tpu as pltpu
from jax.sharding import PartitionSpec as P

L = 100
FOLD = 8
STEPS = -(-L // FOLD)
RIM = 128
LANES = 256
SUB = 5
SLACK = 3
MESH = pl.DeviceIdType.MESH
VMEM = pl.BlockSpec(memory_space=pltpu.VMEM)
SMEM = pl.BlockSpec(memory_space=pltpu.SMEM)


def detect_kernel(pairs, peers, per_batch, owner_ref, x_ref, index_ref, corr_ref, out_aux_ref,
                  own, rim, from_l, from_r, to_r, to_l, block, stack, weights, part, aux, got, got_aux,
                  keep_sem, rim_sem, swap_s, swap_r, rs, rr, ls, lr, s1, r1, s2, r2, s3, r3):
    tm, c = lax.axis_index("tm"), lax.axis_index("chan")
    p, h = tm // 2, tm % 2
    peer = tm + 1 - 2 * h
    half, width = own.shape[1:]
    rows = half // SUB
    batches = index_ref.shape[0]
    chunks = batches * SUB
    span = stack.shape[1]
    reach = part.shape[2]
    deep = part.shape[1]
    groups = peers // batches
    team = 2 * peers
    me = h * peers + c
    has_l, has_r = p > 0, p < pairs - 1

    def member(i):
        m = lax.rem(me + i, team)
        return {"tm": tm - h + m // peers, "chan": m % peers}

    barrier = pltpu.get_barrier_semaphore()
    for i in range(1, team):
        pl.semaphore_signal(barrier, inc=1, device_id=member(i), device_id_type=MESH)

    @pl.when(has_l)
    def _():
        pl.semaphore_signal(barrier, inc=1, device_id={"tm": tm - 2}, device_id_type=MESH)

    @pl.when(has_r)
    def _():
        pl.semaphore_signal(barrier, inc=1, device_id={"tm": tm + 2}, device_id_type=MESH)

    pl.semaphore_wait(barrier, team - 1 + has_l.astype(jnp.int32) + has_r.astype(jnp.int32))

    def swap(q):
        return pltpu.make_async_remote_copy(
            src_ref=x_ref.at[pl.ds(pl.multiple_of((1 - h) * half + q * rows, 16), rows)],
            dst_ref=own.at[h, pl.ds(pl.multiple_of(q * rows, 16), rows)],
            send_sem=swap_s.at[q], recv_sem=swap_r.at[q],
            device_id={"tm": peer}, device_id_type=MESH)

    def swapped(q):
        return pltpu.make_async_remote_copy(
            src_ref=x_ref.at[pl.ds(pl.multiple_of((1 - h) * half + q * rows, 16), rows)],
            dst_ref=own.at[1 - h, pl.ds(pl.multiple_of(q * rows, 16), rows)],
            send_sem=swap_s.at[q], recv_sem=swap_r.at[q],
            device_id={"tm": peer}, device_id_type=MESH)

    def send_swap(q, carry):
        swap(q).start()
        return carry

    lax.fori_loop(0, SUB, send_swap, 0)
    keep = pltpu.make_async_copy(
        x_ref.at[pl.ds(pl.multiple_of(h * half, 16), half)], own.at[h], keep_sem)
    keep.start()
    keep.wait()

    @pl.when(jnp.logical_not(has_l))
    def _():
        from_l[...] = jnp.zeros_like(from_l)

    @pl.when(jnp.logical_not(has_r))
    def _():
        from_r[...] = jnp.zeros_like(from_r)
        rim[...] = jnp.zeros_like(rim)

    rim_copy = pltpu.make_async_remote_copy(
        src_ref=own.at[0, :, pl.ds(0, RIM)], dst_ref=rim,
        send_sem=rim_sem.at[0], recv_sem=rim_sem.at[1],
        device_id={"tm": tm - 2}, device_id_type=MESH)

    def right(i):
        return pltpu.make_async_remote_copy(
            src_ref=to_r.at[i], dst_ref=from_l.at[i], send_sem=rs.at[i], recv_sem=rr.at[i],
            device_id={"tm": tm + 2}, device_id_type=MESH)

    def left(i):
        return pltpu.make_async_remote_copy(
            src_ref=to_l.at[i], dst_ref=from_r.at[i], send_sem=ls.at[i], recv_sem=lr.at[i],
            device_id={"tm": tm - 2}, device_id_type=MESH)

    def mine(i):
        who = owner_ref[i // SUB]
        at = pl.ds(pl.multiple_of((i % SUB) * rows, 16), rows)
        return who, jnp.where(who % 2 == 0, own[0, at, :], own[1, at, :])

    def build():
        @pl.when(has_r)
        def _():
            rim_copy.wait_recv()

        stack[:half, :width] = own[0]
        stack[:half, width:2 * width] = own[1]
        stack[:half, 2 * width:] = rim[...]
        wide = stack[:half].astype(jnp.float32)
        for j in range(1, FOLD):
            stack[j * half:(j + 1) * half] = pltpu.roll(wide, span - j, 1).astype(jnp.bfloat16)
        sums = {1: jnp.broadcast_to(jnp.sum(wide * wide, axis=0, keepdims=True), (8, span))}
        n = 1
        while 2 * n <= L:
            sums[2 * n] = sums[n] + pltpu.roll(sums[n], span - n, 1)
            n *= 2
        done, total = 0, None
        for n in sorted(sums, reverse=True):
            if n & L:
                term = sums[n] if done == 0 else pltpu.roll(sums[n], span - done, 1)
                total = term if total is None else total + term
                done += n
        aux[0, :, :width] = total[:1, :width]
        aux[1, :, :width] = total[:1, width:2 * width]

    def piece(chan, hh):
        return pltpu.make_async_remote_copy(
            src_ref=part.at[chan, :, pl.ds(hh * width, width)],
            dst_ref=got.at[me], send_sem=s1.at[chan, hh], recv_sem=r1.at[me],
            device_id={"tm": tm - h + hh, "chan": chan}, device_id_type=MESH)

    def piece_from(i):
        whose = lax.rem(me + team - i, team)
        return pltpu.make_async_remote_copy(
            src_ref=part.at[0, :, pl.ds(0, width)],
            dst_ref=got.at[whose], send_sem=s1.at[0, 0], recv_sem=r1.at[whose],
            device_id=member(i), device_id_type=MESH)

    def other(chan, hh):
        return jnp.logical_or(chan != c, hh != h)

    def compute(b):
        for q in range(SUB):
            i = b * SUB + q
            who, value = mine(i)
            far = jnp.where(who // 2 < p, from_l[i], from_r[i])
            block[q * rows:(q + 1) * rows] = jnp.where(who // 2 == p, value, far)
        row = lax.broadcasted_iota(jnp.int32, (width, LANES), 0)
        index = index_ref[b]
        norm = jnp.zeros((1, LANES), jnp.float32)
        for j in range(FOLD):
            hot = jnp.where(row == index[j:j + 1], 1.0, 0.0).astype(jnp.bfloat16)
            cut = jnp.dot(block[...], hot, preferred_element_type=jnp.float32)
            norm = norm + jnp.sum(cut * cut, axis=0, keepdims=True)
            weights[j * half:(j + 1) * half] = cut.astype(jnp.bfloat16)
        at = pl.ds(pl.multiple_of(width + b * LANES, 128), LANES)
        aux[0, :, at] = norm
        aux[1, :, at] = norm
        turned = weights[...].T[:STEPS * per_batch]
        grid = jnp.dot(turned, stack[...], preferred_element_type=jnp.float32)
        acc = grid[:per_batch]
        for s in range(1, STEPS):
            acc = acc + pltpu.roll(grid[s * per_batch:(s + 1) * per_batch], span - s * FOLD, 1)
        for k in range(groups):
            part[b * groups + k] = acc[k * deep:(k + 1) * deep, :reach]
        for k in range(groups):
            for hh in range(2):
                chan = b * groups + k

                @pl.when(other(chan, hh))
                def _():
                    piece(chan, hh).start()

    def tick(t, carry):
        @pl.when(t < SUB)
        def _():
            swapped(t).wait_recv()

        @pl.when(jnp.logical_and(t == SUB, has_l))
        def _():
            rim_copy.start()

        i = t - p * SLACK

        @pl.when(jnp.logical_and(i >= 0, i < chunks))
        def _():
            @pl.when(has_l)
            def _():
                right(i).wait_recv()

            @pl.when(has_r)
            def _():
                who, value = mine(i)
                to_r[i] = jnp.where(who // 2 == p, value, from_l[i])
                right(i).start()

        k = t - (pairs - 1 - p) * SLACK

        @pl.when(jnp.logical_and(k >= 0, k < chunks))
        def _():
            @pl.when(has_r)
            def _():
                left(k).wait_recv()

            @pl.when(has_l)
            def _():
                who, value = mine(k)
                to_l[k] = jnp.where(who // 2 == p, value, from_r[k])
                left(k).start()

        @pl.when(t == SUB + 2)
        def _():
            build()

        ready = t + 1 - SUB - SLACK * jnp.maximum(p, pairs - 1 - p)

        @pl.when(jnp.logical_and(ready >= 0, lax.rem(ready + chunks * SUB, SUB) == 0))
        def _():
            @pl.when(ready < chunks)
            def _():
                compute(ready // SUB)

        return carry

    lax.fori_loop(0, chunks + (pairs - 1) * SLACK, tick, 0)

    def extra(i):
        return pltpu.make_async_remote_copy(
            src_ref=aux.at[lax.rem(me + i, team) // peers], dst_ref=got_aux.at[me],
            send_sem=s2.at[i], recv_sem=r2.at[i], device_id=member(i), device_id_type=MESH)

    def extra_from(i):
        whose = lax.rem(me + team - i, team)
        return pltpu.make_async_remote_copy(
            src_ref=aux.at[0], dst_ref=got_aux.at[whose], send_sem=s2.at[i],
            recv_sem=r2.at[i], device_id=member(i), device_id_type=MESH)

    def share(i):
        return pltpu.make_async_remote_copy(
            src_ref=corr_ref.at[c], dst_ref=corr_ref.at[c], send_sem=s3.at[i], recv_sem=r3.at[i],
            device_id={"tm": tm, "chan": lax.rem(c + i, peers)}, device_id_type=MESH)

    def arriving(i):
        whose = lax.rem(c + peers - i, peers)
        return pltpu.make_async_remote_copy(
            src_ref=corr_ref.at[whose], dst_ref=corr_ref.at[whose], send_sem=s3.at[i],
            recv_sem=r3.at[i], device_id={"tm": tm, "chan": whose}, device_id_type=MESH)

    for i in range(1, team):
        extra(i).start()
    got[me] = part[c, :, pl.ds(pl.multiple_of(h * width, 128), width)]
    for i in range(1, team):
        piece_from(i).wait_recv()
    total = got[0]
    for i in range(1, team):
        total = total + got[i]
    corr_ref[c] = total
    for i in range(1, peers):
        share(i).start()
    got_aux[me] = aux[h]
    for i in range(1, team):
        extra_from(i).wait_recv()
    both = got_aux[0]
    for i in range(1, team):
        both = both + got_aux[i]
    out_aux_ref[...] = both
    for i in range(1, peers):
        arriving(i).wait_recv()
    for i in range(1, peers):
        share(i).wait_send()
    for i in range(1, team):
        extra(i).wait_send()
    for chan in range(peers):
        for hh in range(2):
            @pl.when(other(chan, hh))
            def _():
                piece(chan, hh).wait_send()

    def drain(i, carry):
        @pl.when(has_r)
        def _():
            right(i).wait_send()

        @pl.when(has_l)
        def _():
            left(i).wait_send()

        return carry

    lax.fori_loop(0, chunks, drain, 0)

    def drain_swap(q, carry):
        swap(q).wait_send()
        return carry

    lax.fori_loop(0, SUB, drain_swap, 0)

    @pl.when(has_l)
    def _():
        rim_copy.wait_send()


def detect(owner, record, index, pairs, peers, per_batch):
    channels, samples = record.shape
    batches = index.shape[0]
    half = channels // 2
    chunks = batches * SUB
    span = 2 * samples + RIM
    deep = batches * per_batch // peers
    team = 2 * peers
    wide = samples + batches * LANES
    slots = pltpu.VMEM((chunks, half // SUB, samples), record.dtype)
    dma = pltpu.SemaphoreType.DMA
    sems = dma((chunks,))
    many, few = dma((team,)), dma((peers,))
    return pl.pallas_call(
        functools.partial(detect_kernel, pairs, peers, per_batch),
        out_shape=(jax.ShapeDtypeStruct((peers, deep, samples), jnp.float32),
                   jax.ShapeDtypeStruct((1, wide), jnp.float32)),
        in_specs=[SMEM, VMEM, VMEM],
        out_specs=(VMEM, VMEM),
        scratch_shapes=[pltpu.VMEM((2, half, samples), record.dtype),
                        pltpu.VMEM((half, RIM), record.dtype),
                        slots, slots, slots, slots,
                        pltpu.VMEM((half, samples), record.dtype),
                        pltpu.VMEM((FOLD * half, span), record.dtype),
                        pltpu.VMEM((FOLD * half, LANES), record.dtype),
                        pltpu.VMEM((peers, deep, 2 * samples), jnp.float32),
                        pltpu.VMEM((2, 1, wide), jnp.float32),
                        pltpu.VMEM((team, deep, samples), jnp.float32),
                        pltpu.VMEM((team, 1, wide), jnp.float32),
                        dma, dma((2,)), dma((SUB,)), dma((SUB,)), sems, sems, sems, sems,
                        dma((peers, 2)), many, many, many, few, few],
        compiler_params=pltpu.CompilerParams(
            collective_id=0, has_side_effects=True, vmem_limit_bytes=50 << 20),
        name="detect",
    )(owner, record, index)


def on_device(pairs, peers, record, owner, offsets):
    samples = record.shape[1]
    batches, per_batch = offsets.shape
    lane = jnp.arange(LANES)
    tap = FOLD * (lane // per_batch)[None, :] + jnp.arange(FOLD)[:, None]
    start = offsets[:, lane % per_batch]
    index = jnp.where(tap[None] < L, start[:, None, :] + tap[None], -1).astype(jnp.int32)

    total, aux = detect(owner, record, index, pairs, peers, per_batch)
    energy = aux[0, :samples]
    norms = aux[0, samples:].reshape(batches, LANES // per_batch, per_batch).sum(axis=1)
    total = total.reshape(batches, per_batch, samples)
    return total / jnp.sqrt((energy + 1e-05)[None, None, :] * norms[:, :, None])


def solution(mesh):
    run = functools.partial(on_device, mesh.shape["tm"] // 2, mesh.shape["chan"])
    return jax.shard_map(
        run, mesh=mesh, in_specs=(P("chan", "tm"), P(), P()),
        out_specs=P(None, None, "tm"), check_vma=False)
```

```python
import functools

import jax
import jax.numpy as jnp
from jax import lax
from jax.experimental import pallas as pl
from jax.experimental.pallas import tpu as pltpu
from jax.sharding import PartitionSpec as P

L = 100
FOLD = 8
STEPS = -(-L // FOLD)
RIM = 128
LANES = 256
SUB = 5
SLACK = 3
MESH = pl.DeviceIdType.MESH
VMEM = pl.BlockSpec(memory_space=pltpu.VMEM)
SMEM = pl.BlockSpec(memory_space=pltpu.SMEM)


def detect_kernel(pairs, peers, per_batch, owner_ref, x_ref, index_ref, corr_ref, out_aux_ref,
                  own, rim, from_l, from_r, to_r, to_l, block, stack, weights, part, aux, got, got_aux,
                  keep_sem, rim_sem, swap_s, swap_r, rs, rr, ls, lr, s1, r1, s2, r2, s3, r3):
    tm, c = lax.axis_index("tm"), lax.axis_index("chan")
    p, h = tm // 2, tm % 2
    peer = tm + 1 - 2 * h
    half, width = own.shape[1:]
    rows = half // SUB
    batches = index_ref.shape[0]
    chunks = batches * SUB
    span = stack.shape[1]
    reach = part.shape[2]
    deep = part.shape[1]
    groups = peers // batches
    team = 2 * peers
    me = h * peers + c
    has_l, has_r = p > 0, p < pairs - 1

    def member(i):
        m = lax.rem(me + i, team)
        return {"tm": tm - h + m // peers, "chan": m % peers}

    barrier = pltpu.get_barrier_semaphore()
    for i in range(1, team):
        pl.semaphore_signal(barrier, inc=1, device_id=member(i), device_id_type=MESH)

    @pl.when(has_l)
    def _():
        pl.semaphore_signal(barrier, inc=1, device_id={"tm": tm - 2}, device_id_type=MESH)

    @pl.when(has_r)
    def _():
        pl.semaphore_signal(barrier, inc=1, device_id={"tm": tm + 2}, device_id_type=MESH)

    pl.semaphore_wait(barrier, team - 1 + has_l.astype(jnp.int32) + has_r.astype(jnp.int32))

    def swap(q):
        return pltpu.make_async_remote_copy(
            src_ref=x_ref.at[pl.ds(pl.multiple_of((1 - h) * half + q * rows, 16), rows)],
            dst_ref=own.at[h, pl.ds(pl.multiple_of(q * rows, 16), rows)],
            send_sem=swap_s.at[q], recv_sem=swap_r.at[q],
            device_id={"tm": peer}, device_id_type=MESH)

    def swapped(q):
        return pltpu.make_async_remote_copy(
            src_ref=x_ref.at[pl.ds(pl.multiple_of((1 - h) * half + q * rows, 16), rows)],
            dst_ref=own.at[1 - h, pl.ds(pl.multiple_of(q * rows, 16), rows)],
            send_sem=swap_s.at[q], recv_sem=swap_r.at[q],
            device_id={"tm": peer}, device_id_type=MESH)

    def send_swap(q, carry):
        swap(q).start()
        return carry

    lax.fori_loop(0, SUB, send_swap, 0)
    keep = pltpu.make_async_copy(
        x_ref.at[pl.ds(pl.multiple_of(h * half, 16), half)], own.at[h], keep_sem)
    keep.start()
    keep.wait()

    @pl.when(jnp.logical_not(has_l))
    def _():
        from_l[...] = jnp.zeros_like(from_l)

    @pl.when(jnp.logical_not(has_r))
    def _():
        from_r[...] = jnp.zeros_like(from_r)
        rim[...] = jnp.zeros_like(rim)

    rim_copy = pltpu.make_async_remote_copy(
        src_ref=own.at[0, :, pl.ds(0, RIM)], dst_ref=rim,
        send_sem=rim_sem.at[0], recv_sem=rim_sem.at[1],
        device_id={"tm": tm - 2}, device_id_type=MESH)

    def right(i):
        return pltpu.make_async_remote_copy(
            src_ref=to_r.at[i], dst_ref=from_l.at[i], send_sem=rs.at[i], recv_sem=rr.at[i],
            device_id={"tm": tm + 2}, device_id_type=MESH)

    def left(i):
        return pltpu.make_async_remote_copy(
            src_ref=to_l.at[i], dst_ref=from_r.at[i], send_sem=ls.at[i], recv_sem=lr.at[i],
            device_id={"tm": tm - 2}, device_id_type=MESH)

    def mine(i):
        who = owner_ref[i // SUB]
        at = pl.ds(pl.multiple_of((i % SUB) * rows, 16), rows)
        return who, jnp.where(who % 2 == 0, own[0, at, :], own[1, at, :])

    def build():
        @pl.when(has_r)
        def _():
            rim_copy.wait_recv()

        stack[:half, :width] = own[0]
        stack[:half, width:2 * width] = own[1]
        stack[:half, 2 * width:] = rim[...]
        wide = stack[:half].astype(jnp.float32)
        for j in range(1, FOLD):
            stack[j * half:(j + 1) * half] = pltpu.roll(wide, span - j, 1).astype(jnp.bfloat16)
        sums = {1: jnp.broadcast_to(jnp.sum(wide * wide, axis=0, keepdims=True), (8, span))}
        n = 1
        while 2 * n <= L:
            sums[2 * n] = sums[n] + pltpu.roll(sums[n], span - n, 1)
            n *= 2
        done, total = 0, None
        for n in sorted(sums, reverse=True):
            if n & L:
                term = sums[n] if done == 0 else pltpu.roll(sums[n], span - done, 1)
                total = term if total is None else total + term
                done += n
        aux[0, :, :width] = total[:1, :width]
        aux[1, :, :width] = total[:1, width:2 * width]

    def piece(chan, hh):
        return pltpu.make_async_remote_copy(
            src_ref=part.at[chan, :, pl.ds(hh * width, width)],
            dst_ref=got.at[me], send_sem=s1.at[chan, hh], recv_sem=r1.at[me],
            device_id={"tm": tm - h + hh, "chan": chan}, device_id_type=MESH)

    def piece_from(i):
        whose = lax.rem(me + team - i, team)
        return pltpu.make_async_remote_copy(
            src_ref=part.at[0, :, pl.ds(0, width)],
            dst_ref=got.at[whose], send_sem=s1.at[0, 0], recv_sem=r1.at[whose],
            device_id=member(i), device_id_type=MESH)

    def other(chan, hh):
        return jnp.logical_or(chan != c, hh != h)

    def compute(b):
        for q in range(SUB):
            i = b * SUB + q
            who, value = mine(i)
            far = jnp.where(who // 2 < p, from_l[i], from_r[i])
            block[q * rows:(q + 1) * rows] = jnp.where(who // 2 == p, value, far)
        row = lax.broadcasted_iota(jnp.int32, (width, LANES), 0)
        index = index_ref[b]
        norm = jnp.zeros((1, LANES), jnp.float32)
        for j in range(FOLD):
            hot = jnp.where(row == index[j:j + 1], 1.0, 0.0).astype(jnp.bfloat16)
            cut = jnp.dot(block[...], hot, preferred_element_type=jnp.float32)
            norm = norm + jnp.sum(cut * cut, axis=0, keepdims=True)
            weights[j * half:(j + 1) * half] = cut.astype(jnp.bfloat16)
        at = pl.ds(pl.multiple_of(width + b * LANES, 128), LANES)
        aux[0, :, at] = norm
        aux[1, :, at] = norm
        turned = weights[...].T[:STEPS * per_batch]
        grid = jnp.dot(turned, stack[...], preferred_element_type=jnp.float32)
        acc = grid[:per_batch]
        for s in range(1, STEPS):
            acc = acc + pltpu.roll(grid[s * per_batch:(s + 1) * per_batch], span - s * FOLD, 1)
        for k in range(groups):
            part[b * groups + k] = acc[k * deep:(k + 1) * deep, :reach]
        for k in range(groups):
            for hh in range(2):
                chan = b * groups + k

                @pl.when(other(chan, hh))
                def _():
                    piece(chan, hh).start()

    def share(i):
        return pltpu.make_async_remote_copy(
            src_ref=corr_ref.at[c], dst_ref=corr_ref.at[c], send_sem=s3.at[i], recv_sem=r3.at[i],
            device_id={"tm": tm, "chan": lax.rem(c + i, peers)}, device_id_type=MESH)

    def arriving(i):
        whose = lax.rem(c + peers - i, peers)
        return pltpu.make_async_remote_copy(
            src_ref=corr_ref.at[whose], dst_ref=corr_ref.at[whose], send_sem=s3.at[i],
            recv_sem=r3.at[i], device_id={"tm": tm, "chan": whose}, device_id_type=MESH)

    def finish():
        got[me] = part[c, :, pl.ds(pl.multiple_of(h * width, 128), width)]
        for i in range(1, team):
            piece_from(i).wait_recv()
        total = got[0]
        for i in range(1, team):
            total = total + got[i]
        corr_ref[c] = total
        for i in range(1, peers):
            share(i).start()

    def tick(t, carry):
        @pl.when(t < SUB)
        def _():
            swapped(t).wait_recv()

        @pl.when(jnp.logical_and(t == SUB, has_l))
        def _():
            rim_copy.start()

        i = t - p * SLACK

        @pl.when(jnp.logical_and(i >= 0, i < chunks))
        def _():
            @pl.when(has_l)
            def _():
                right(i).wait_recv()

            @pl.when(has_r)
            def _():
                who, value = mine(i)
                to_r[i] = jnp.where(who // 2 == p, value, from_l[i])
                right(i).start()

        k = t - (pairs - 1 - p) * SLACK

        @pl.when(jnp.logical_and(k >= 0, k < chunks))
        def _():
            @pl.when(has_r)
            def _():
                left(k).wait_recv()

            @pl.when(has_l)
            def _():
                who, value = mine(k)
                to_l[k] = jnp.where(who // 2 == p, value, from_r[k])
                left(k).start()

        @pl.when(t == SUB + 2)
        def _():
            build()

        ready = t + 1 - SUB - SLACK * jnp.maximum(p, pairs - 1 - p)

        @pl.when(jnp.logical_and(ready >= 0, lax.rem(ready + chunks * SUB, SUB) == 0))
        def _():
            @pl.when(ready < chunks)
            def _():
                compute(ready // SUB)

                @pl.when(ready // SUB == c // groups + 1)
                def _():
                    finish()

        return carry

    lax.fori_loop(0, chunks + (pairs - 1) * SLACK, tick, 0)

    def extra(i):
        return pltpu.make_async_remote_copy(
            src_ref=aux.at[lax.rem(me + i, team) // peers], dst_ref=got_aux.at[me],
            send_sem=s2.at[i], recv_sem=r2.at[i], device_id=member(i), device_id_type=MESH)

    def extra_from(i):
        whose = lax.rem(me + team - i, team)
        return pltpu.make_async_remote_copy(
            src_ref=aux.at[0], dst_ref=got_aux.at[whose], send_sem=s2.at[i],
            recv_sem=r2.at[i], device_id=member(i), device_id_type=MESH)

    for i in range(1, team):
        extra(i).start()
    @pl.when(c // groups == batches - 1)
    def _():
        finish()

    got_aux[me] = aux[h]
    for i in range(1, team):
        extra_from(i).wait_recv()
    both = got_aux[0]
    for i in range(1, team):
        both = both + got_aux[i]
    out_aux_ref[...] = both
    for i in range(1, peers):
        arriving(i).wait_recv()
    for i in range(1, peers):
        share(i).wait_send()
    for i in range(1, team):
        extra(i).wait_send()
    for chan in range(peers):
        for hh in range(2):
            @pl.when(other(chan, hh))
            def _():
                piece(chan, hh).wait_send()

    def drain(i, carry):
        @pl.when(has_r)
        def _():
            right(i).wait_send()

        @pl.when(has_l)
        def _():
            left(i).wait_send()

        return carry

    lax.fori_loop(0, chunks, drain, 0)

    def drain_swap(q, carry):
        swap(q).wait_send()
        return carry

    lax.fori_loop(0, SUB, drain_swap, 0)

    @pl.when(has_l)
    def _():
        rim_copy.wait_send()


def detect(owner, record, index, pairs, peers, per_batch):
    channels, samples = record.shape
    batches = index.shape[0]
    half = channels // 2
    chunks = batches * SUB
    span = 2 * samples + RIM
    deep = batches * per_batch // peers
    team = 2 * peers
    wide = samples + batches * LANES
    slots = pltpu.VMEM((chunks, half // SUB, samples), record.dtype)
    dma = pltpu.SemaphoreType.DMA
    sems = dma((chunks,))
    many, few = dma((team,)), dma((peers,))
    return pl.pallas_call(
        functools.partial(detect_kernel, pairs, peers, per_batch),
        out_shape=(jax.ShapeDtypeStruct((peers, deep, samples), jnp.float32),
                   jax.ShapeDtypeStruct((1, wide), jnp.float32)),
        in_specs=[SMEM, pl.BlockSpec(memory_space=pl.ANY), VMEM],
        out_specs=(VMEM, VMEM),
        scratch_shapes=[pltpu.VMEM((2, half, samples), record.dtype),
                        pltpu.VMEM((half, RIM), record.dtype),
                        slots, slots, slots, slots,
                        pltpu.VMEM((half, samples), record.dtype),
                        pltpu.VMEM((FOLD * half, span), record.dtype),
                        pltpu.VMEM((FOLD * half, LANES), record.dtype),
                        pltpu.VMEM((peers, deep, 2 * samples), jnp.float32),
                        pltpu.VMEM((2, 1, wide), jnp.float32),
                        pltpu.VMEM((team, deep, samples), jnp.float32),
                        pltpu.VMEM((team, 1, wide), jnp.float32),
                        dma, dma((2,)), dma((SUB,)), dma((SUB,)), sems, sems, sems, sems,
                        dma((peers, 2)), many, many, many, few, few],
        compiler_params=pltpu.CompilerParams(
            collective_id=0, has_side_effects=True, vmem_limit_bytes=50 << 20),
        name="detect",
    )(owner, record, index)


def on_device(pairs, peers, record, owner, offsets):
    samples = record.shape[1]
    batches, per_batch = offsets.shape
    lane = jnp.arange(LANES)
    tap = FOLD * (lane // per_batch)[None, :] + jnp.arange(FOLD)[:, None]
    start = jnp.tile(offsets, (1, LANES // per_batch))
    index = jnp.where(tap[None] < L, start[:, None, :] + tap[None], -1).astype(jnp.int32)

    total, aux = detect(owner, record, index, pairs, peers, per_batch)
    energy = aux[0, :samples]
    norms = aux[0, samples:].reshape(batches, LANES // per_batch, per_batch).sum(axis=1)
    total = total.reshape(batches, per_batch, samples)
    return total / jnp.sqrt((energy + 1e-05)[None, None, :] * norms[:, :, None])


def solution(mesh):
    run = functools.partial(on_device, mesh.shape["tm"] // 2, mesh.shape["chan"])
    return jax.shard_map(
        run, mesh=mesh, in_specs=(P("chan", "tm"), P(), P()),
        out_specs=P(None, None, "tm"), check_vma=False)
```

```python
import functools

import jax
import jax.numpy as jnp
from jax import lax
from jax.experimental import pallas as pl
from jax.experimental.pallas import tpu as pltpu
from jax.sharding import PartitionSpec as P

L = 100
FOLD = 8
STEPS = -(-L // FOLD)
RIM = 128
LANES = 256
SUB = 5
SLACK = 3
MESH = pl.DeviceIdType.MESH
VMEM = pl.BlockSpec(memory_space=pltpu.VMEM)
SMEM = pl.BlockSpec(memory_space=pltpu.SMEM)


def detect_kernel(pairs, peers, per_batch, owner_ref, x_ref, index_ref, corr_ref, out_aux_ref,
                  own, rim, from_l, from_r, to_r, to_l, block, stack, weights, part, aux, got, got_aux,
                  keep_sem, rim_sem, swap_s, swap_r, rs, rr, ls, lr, s1, r1, s2, r2, s3, r3):
    tm, c = lax.axis_index("tm"), lax.axis_index("chan")
    p, h = tm // 2, tm % 2
    peer = tm + 1 - 2 * h
    half, width = own.shape[1:]
    rows = half // SUB
    batches = index_ref.shape[0]
    chunks = batches * SUB
    span = stack.shape[1]
    reach = part.shape[2]
    deep = part.shape[1]
    groups = peers // batches
    team = 2 * peers
    me = h * peers + c
    has_l, has_r = p > 0, p < pairs - 1

    def member(i):
        m = lax.rem(me + i, team)
        return {"tm": tm - h + m // peers, "chan": m % peers}

    barrier = pltpu.get_barrier_semaphore()
    for i in range(1, team):
        pl.semaphore_signal(barrier, inc=1, device_id=member(i), device_id_type=MESH)

    @pl.when(has_l)
    def _():
        pl.semaphore_signal(barrier, inc=1, device_id={"tm": tm - 2}, device_id_type=MESH)

    @pl.when(has_r)
    def _():
        pl.semaphore_signal(barrier, inc=1, device_id={"tm": tm + 2}, device_id_type=MESH)

    pl.semaphore_wait(barrier, team - 1 + has_l.astype(jnp.int32) + has_r.astype(jnp.int32))

    def swap(q):
        return pltpu.make_async_remote_copy(
            src_ref=x_ref.at[pl.ds(pl.multiple_of((1 - h) * half + q * rows, 16), rows)],
            dst_ref=own.at[h, pl.ds(pl.multiple_of(q * rows, 16), rows)],
            send_sem=swap_s.at[q], recv_sem=swap_r.at[q],
            device_id={"tm": peer}, device_id_type=MESH)

    def swapped(q):
        return pltpu.make_async_remote_copy(
            src_ref=x_ref.at[pl.ds(pl.multiple_of((1 - h) * half + q * rows, 16), rows)],
            dst_ref=own.at[1 - h, pl.ds(pl.multiple_of(q * rows, 16), rows)],
            send_sem=swap_s.at[q], recv_sem=swap_r.at[q],
            device_id={"tm": peer}, device_id_type=MESH)

    def send_swap(q, carry):
        swap(q).start()
        return carry

    lax.fori_loop(0, SUB, send_swap, 0)
    keep = pltpu.make_async_copy(
        x_ref.at[pl.ds(pl.multiple_of(h * half, 16), half)], own.at[h], keep_sem)
    keep.start()
    keep.wait()

    @pl.when(jnp.logical_not(has_l))
    def _():
        from_l[...] = jnp.zeros_like(from_l)

    @pl.when(jnp.logical_not(has_r))
    def _():
        from_r[...] = jnp.zeros_like(from_r)
        rim[...] = jnp.zeros_like(rim)

    rim_copy = pltpu.make_async_remote_copy(
        src_ref=own.at[0, :, pl.ds(0, RIM)], dst_ref=rim,
        send_sem=rim_sem.at[0], recv_sem=rim_sem.at[1],
        device_id={"tm": tm - 2}, device_id_type=MESH)

    def right(i):
        return pltpu.make_async_remote_copy(
            src_ref=to_r.at[i], dst_ref=from_l.at[i], send_sem=rs.at[i], recv_sem=rr.at[i],
            device_id={"tm": tm + 2}, device_id_type=MESH)

    def left(i):
        return pltpu.make_async_remote_copy(
            src_ref=to_l.at[i], dst_ref=from_r.at[i], send_sem=ls.at[i], recv_sem=lr.at[i],
            device_id={"tm": tm - 2}, device_id_type=MESH)

    def mine(i):
        who = owner_ref[i // SUB]
        at = pl.ds(pl.multiple_of((i % SUB) * rows, 16), rows)
        return who, jnp.where(who % 2 == 0, own[0, at, :], own[1, at, :])

    def build():
        @pl.when(has_r)
        def _():
            rim_copy.wait_recv()

        stack[:half, :width] = own[0]
        stack[:half, width:2 * width] = own[1]
        stack[:half, 2 * width:] = rim[...]
        wide = stack[:half].astype(jnp.float32)
        for j in range(1, FOLD):
            stack[j * half:(j + 1) * half] = pltpu.roll(wide, span - j, 1).astype(jnp.bfloat16)
        sums = {1: jnp.broadcast_to(jnp.sum(wide * wide, axis=0, keepdims=True), (8, span))}
        n = 1
        while 2 * n <= L:
            sums[2 * n] = sums[n] + pltpu.roll(sums[n], span - n, 1)
            n *= 2
        done, total = 0, None
        for n in sorted(sums, reverse=True):
            if n & L:
                term = sums[n] if done == 0 else pltpu.roll(sums[n], span - done, 1)
                total = term if total is None else total + term
                done += n
        aux[0, :, :width] = total[:1, :width]
        aux[1, :, :width] = total[:1, width:2 * width]

    def piece(chan, hh):
        return pltpu.make_async_remote_copy(
            src_ref=part.at[chan, :, pl.ds(hh * width, width)],
            dst_ref=got.at[me], send_sem=s1.at[chan, hh], recv_sem=r1.at[me],
            device_id={"tm": tm - h + hh, "chan": chan}, device_id_type=MESH)

    def piece_from(i):
        whose = lax.rem(me + team - i, team)
        return pltpu.make_async_remote_copy(
            src_ref=part.at[0, :, pl.ds(0, width)],
            dst_ref=got.at[whose], send_sem=s1.at[0, 0], recv_sem=r1.at[whose],
            device_id=member(i), device_id_type=MESH)

    def other(chan, hh):
        return jnp.logical_or(chan != c, hh != h)

    def compute(b):
        for q in range(SUB):
            i = b * SUB + q
            who, value = mine(i)
            far = jnp.where(who // 2 < p, from_l[i], from_r[i])
            block[q * rows:(q + 1) * rows] = jnp.where(who // 2 == p, value, far)
        row = lax.broadcasted_iota(jnp.int32, (width, LANES), 0)
        index = index_ref[b]
        norm = jnp.zeros((1, LANES), jnp.float32)
        for j in range(FOLD):
            hot = jnp.where(row == index[j:j + 1], 1.0, 0.0).astype(jnp.bfloat16)
            cut = jnp.dot(block[...], hot, preferred_element_type=jnp.float32)
            norm = norm + jnp.sum(cut * cut, axis=0, keepdims=True)
            weights[j * half:(j + 1) * half] = cut.astype(jnp.bfloat16)
        at = pl.ds(pl.multiple_of(width + b * LANES, 128), LANES)
        aux[0, :, at] = norm
        aux[1, :, at] = norm
        turned = weights[...].T[:STEPS * per_batch]
        grid = jnp.dot(turned, stack[...], preferred_element_type=jnp.float32)
        acc = grid[:per_batch]
        for s in range(1, STEPS):
            acc = acc + pltpu.roll(grid[s * per_batch:(s + 1) * per_batch], span - s * FOLD, 1)
        for k in range(groups):
            part[b * groups + k] = acc[k * deep:(k + 1) * deep, :reach]
        for k in range(groups):
            for hh in range(2):
                chan = b * groups + k

                @pl.when(other(chan, hh))
                def _():
                    piece(chan, hh).start()

    def share(i):
        return pltpu.make_async_remote_copy(
            src_ref=corr_ref.at[c], dst_ref=corr_ref.at[c], send_sem=s3.at[i], recv_sem=r3.at[i],
            device_id={"tm": tm, "chan": lax.rem(c + i, peers)}, device_id_type=MESH)

    def arriving(i):
        whose = lax.rem(c + peers - i, peers)
        return pltpu.make_async_remote_copy(
            src_ref=corr_ref.at[whose], dst_ref=corr_ref.at[whose], send_sem=s3.at[i],
            recv_sem=r3.at[i], device_id={"tm": tm, "chan": whose}, device_id_type=MESH)

    def finish():
        got[me] = part[c, :, pl.ds(pl.multiple_of(h * width, 128), width)]
        for i in range(1, team):
            piece_from(i).wait_recv()
        total = got[0]
        for i in range(1, team):
            total = total + got[i]
        corr_ref[c] = total
        for i in range(1, peers):
            share(i).start()

    def tick(t, carry):
        @pl.when(t < SUB)
        def _():
            swapped(t).wait_recv()

        @pl.when(jnp.logical_and(t == SUB, has_l))
        def _():
            rim_copy.start()

        i = t - p * SLACK

        @pl.when(jnp.logical_and(i >= 0, i < chunks))
        def _():
            @pl.when(has_l)
            def _():
                right(i).wait_recv()

            @pl.when(has_r)
            def _():
                who, value = mine(i)
                to_r[i] = jnp.where(who // 2 == p, value, from_l[i])
                right(i).start()

        k = t - (pairs - 1 - p) * SLACK

        @pl.when(jnp.logical_and(k >= 0, k < chunks))
        def _():
            @pl.when(has_r)
            def _():
                left(k).wait_recv()

            @pl.when(has_l)
            def _():
                who, value = mine(k)
                to_l[k] = jnp.where(who // 2 == p, value, from_r[k])
                left(k).start()

        @pl.when(t == SUB + 2)
        def _():
            build()

        ready = t + 1 - SUB - SLACK * jnp.maximum(p, pairs - 1 - p)

        @pl.when(jnp.logical_and(ready >= 0, lax.rem(ready + chunks * SUB, SUB) == 0))
        def _():
            @pl.when(ready < chunks)
            def _():
                compute(ready // SUB)

                @pl.when(ready // SUB == c // groups + 1)
                def _():
                    finish()

        return carry

    lax.fori_loop(0, chunks + (pairs - 1) * SLACK, tick, 0)

    def extra(i):
        return pltpu.make_async_remote_copy(
            src_ref=aux.at[lax.rem(me + i, team) // peers], dst_ref=got_aux.at[me],
            send_sem=s2.at[i], recv_sem=r2.at[i], device_id=member(i), device_id_type=MESH)

    def extra_from(i):
        whose = lax.rem(me + team - i, team)
        return pltpu.make_async_remote_copy(
            src_ref=aux.at[0], dst_ref=got_aux.at[whose], send_sem=s2.at[i],
            recv_sem=r2.at[i], device_id=member(i), device_id_type=MESH)

    for i in range(1, team):
        extra(i).start()
    @pl.when(c // groups == batches - 1)
    def _():
        finish()

    got_aux[me] = aux[h]
    for i in range(1, team):
        extra_from(i).wait_recv()
    both = got_aux[0]
    for i in range(1, team):
        both = both + got_aux[i]
    out_aux_ref[...] = both
    for i in range(1, peers):
        arriving(i).wait_recv()
    for i in range(1, peers):
        share(i).wait_send()
    for i in range(1, team):
        extra(i).wait_send()
    for chan in range(peers):
        for hh in range(2):
            @pl.when(other(chan, hh))
            def _():
                piece(chan, hh).wait_send()

    def drain(i, carry):
        @pl.when(has_r)
        def _():
            right(i).wait_send()

        @pl.when(has_l)
        def _():
            left(i).wait_send()

        return carry

    lax.fori_loop(0, chunks, drain, 0)

    def drain_swap(q, carry):
        swap(q).wait_send()
        return carry

    lax.fori_loop(0, SUB, drain_swap, 0)

    @pl.when(has_l)
    def _():
        rim_copy.wait_send()


def detect(owner, record, index, pairs, peers, per_batch):
    channels, samples = record.shape
    batches = index.shape[0]
    half = channels // 2
    chunks = batches * SUB
    span = 2 * samples + RIM
    deep = batches * per_batch // peers
    team = 2 * peers
    wide = samples + batches * LANES
    slots = pltpu.VMEM((chunks, half // SUB, samples), record.dtype)
    dma = pltpu.SemaphoreType.DMA
    sems = dma((chunks,))
    many, few = dma((team,)), dma((peers,))
    return pl.pallas_call(
        functools.partial(detect_kernel, pairs, peers, per_batch),
        out_shape=(jax.ShapeDtypeStruct((peers, deep, samples), jnp.float32),
                   jax.ShapeDtypeStruct((1, wide), jnp.float32)),
        in_specs=[SMEM, pl.BlockSpec(memory_space=pltpu.HBM), VMEM],
        out_specs=(VMEM, VMEM),
        scratch_shapes=[pltpu.VMEM((2, half, samples), record.dtype),
                        pltpu.VMEM((half, RIM), record.dtype),
                        slots, slots, slots, slots,
                        pltpu.VMEM((half, samples), record.dtype),
                        pltpu.VMEM((FOLD * half, span), record.dtype),
                        pltpu.VMEM((FOLD * half, LANES), record.dtype),
                        pltpu.VMEM((peers, deep, 2 * samples), jnp.float32),
                        pltpu.VMEM((2, 1, wide), jnp.float32),
                        pltpu.VMEM((team, deep, samples), jnp.float32),
                        pltpu.VMEM((team, 1, wide), jnp.float32),
                        dma, dma((2,)), dma((SUB,)), dma((SUB,)), sems, sems, sems, sems,
                        dma((peers, 2)), many, many, many, few, few],
        compiler_params=pltpu.CompilerParams(
            collective_id=0, has_side_effects=True, vmem_limit_bytes=50 << 20),
        name="detect",
    )(owner, record, index)


def on_device(pairs, peers, record, owner, offsets):
    samples = record.shape[1]
    batches, per_batch = offsets.shape
    lane = jnp.arange(LANES)
    tap = FOLD * (lane // per_batch)[None, :] + jnp.arange(FOLD)[:, None]
    start = jnp.tile(offsets, (1, LANES // per_batch))
    index = jnp.where(tap[None] < L, start[:, None, :] + tap[None], -1).astype(jnp.int32)

    total, aux = detect(owner, record, index, pairs, peers, per_batch)
    energy = aux[0, :samples]
    norms = aux[0, samples:].reshape(batches, LANES // per_batch, per_batch).sum(axis=1)
    total = total.reshape(batches, per_batch, samples)
    return total / jnp.sqrt((energy + 1e-05)[None, None, :] * norms[:, :, None])


def solution(mesh):
    run = functools.partial(on_device, mesh.shape["tm"] // 2, mesh.shape["chan"])
    return jax.shard_map(
        run, mesh=mesh, in_specs=(P("chan", "tm"), P(), P()),
        out_specs=P(None, None, "tm"), check_vma=False)
```
